512 devices in a mesh: row: 32 (over z, x), col: 16 (over y, core).
Axes of the slice: x: 4, y: 8, z: 8, core: 2. Of those that a mesh axis runs over, the one named last changes fastest.
Arguments:
- features: bfloat16 [65536, 128], P(('row', 'col')), may hold values from -6 to 6
- cotangent: bfloat16 [65536, 128], P(('row', 'col')), may hold values from -6 to 6
- self_weight: bfloat16 [128, 128], replicated, may hold values from -0.5 to 0.5
- neigh_weight: bfloat16 [128, 128], replicated, may hold values from -0.5 to 0.5
- degrees: int32 [65536], P(('row', 'col')), may hold values from 512 to 2048
- adjacency: int32 [32, 16, 64, 128, 128], P('row', 'col'), may hold values 0 or 1
- tile_rows: int32 [32, 16, 64], P('row', 'col'), may hold values from 0 to 31
- tile_cols: int32 [32, 16, 64], P('row', 'col'), may hold values from 0 to 15
- tile_count: int32 [32, 16], P('row', 'col'), may hold values from 32 to 64, as said below
Outputs:
- hidden: bfloat16 [65536, 128], P(('row', 'col'))
- grad_features: bfloat16 [65536, 128], P(('row', 'col'))
- grad_self: float32 [128, 128], replicated
- grad_neigh: float32 [128, 128], replicated
The draws below stay inside these ranges and needn't reach their ends.
Inputs may be any that keep to these rules, and one draw needn't show every extreme that they name: `tile_count`: each device has between 64 // 2 (at least 1) and 64 live slots; in every draw some device has exactly 64. `tile_rows`: only a device's first tile_count slots are live; places may repeat. `tile_cols`: only a device's first tile_count slots are live; places may repeat.
All inputs are finite; a program needn't handle non-finite values. No bound on the sum of `adjacency` on one device may be relied on, other than what follows from the above.
Results may differ from the reference program's by a relative error of at most 0.024.
Values may be sent and summed in bfloat16 or wider, within the bound.
No kernel may reach another device: no remote copies, remote signals or barrier semaphores. Data moves between devices by JAX's collectives and lax.ppermute only.
A program may use at most 64 MiB of HBM per device.

```python
import jax
import jax.numpy as jnp
from jax import lax

F = 128
BLK = 128
BPD = 1
K = 64
ROWB = 32
COLB = 16
NODES = 65536
N_ROW = 32
N_COL = 16


def draw_tile_count(key, part):
    key = jax.random.fold_in(key, 7)
    first_key, second_key = jax.random.split(key)
    counts = jax.random.randint(first_key, (N_ROW * N_COL,), max(1, K // 2), K + 1, dtype=jnp.int32)
    chosen = jax.random.randint(second_key, (), 0, N_ROW * N_COL, dtype=jnp.int32)
    positions = jnp.arange(N_ROW * N_COL, dtype=jnp.int32)
    counts = jnp.where(positions == chosen, K, counts).astype(jnp.int32)
    return counts.reshape(N_ROW, N_COL)


def set_ends(array, key, low, top_value):
    longest = array.shape.index(max(array.shape))
    spots = []
    for shift in (0, 1):
        where = [jax.random.randint(jax.random.fold_in(key, axis), (), 0, length) for axis, length in enumerate(array.shape)]
        where[longest] = (where[longest] + shift) % array.shape[longest]
        spots.append(tuple(where))
    return array.at[spots[0]].set(low).at[spots[1]].set(top_value)


def steps_of(key, dims, cuts, low, largest):
    loudness = 1.0
    for axis_at, parts in cuts:
        steps = jax.random.uniform(jax.random.fold_in(jax.random.fold_in(key, 6), axis_at), (parts,), jnp.float32, low / len(cuts), largest / len(cuts))
        loudness = loudness * jnp.repeat(jnp.exp(steps), dims[axis_at] // parts).reshape((-1,) + (1,) * (len(dims) - 1 - axis_at))
    return loudness


def noise(rng, dims, scale, bound, cuts=(), held_as=jnp.bfloat16):
    array = jax.random.normal(rng, dims, jnp.float32) * scale
    if len(cuts) > 0:
        array = steps_of(rng, dims, cuts, -0.22, 0.18) * array
    return jnp.clip(array, min=-bound, max=bound).astype(held_as)


def setup_inputs(seed: int = 0) -> dict:
    key_of = jax.random.split(jax.random.key(seed), 10)
    return {
        "features": noise(key_of[0], (NODES, F), 1.0, 6.0, ((0, 512),)),
        "cotangent": noise(key_of[1], (NODES, F), 1.0, 6.0, ((0, 512),)),
        "self_weight": noise(key_of[2], (F, F), F ** -0.5, 0.5),
        "neigh_weight": noise(key_of[3], (F, F), F ** -0.5, 0.5),
        "degrees": set_ends(jax.random.randint(key_of[4], (NODES,), max(1, K * BLK // (16 * BPD)), K * BLK // (4 * BPD) + 1), jax.random.fold_in(key_of[4], 1), max(1, K * BLK // (16 * BPD)), (K * BLK // (4 * BPD) + 1) - 1).astype(jnp.int32),
        "adjacency": set_ends((jax.random.randint(key_of[5], (N_ROW, N_COL, K, BLK, BLK), 0, 8) < 1).astype(jnp.int32), jax.random.fold_in(key_of[5], 1), 0, 1),
        "tile_rows": set_ends(jax.random.randint(key_of[6], (N_ROW, N_COL, K), 0, ROWB), jax.random.fold_in(key_of[6], 1), 0, ROWB - 1).astype(jnp.int32),
        "tile_cols": set_ends(jax.random.randint(key_of[7], (N_ROW, N_COL, K), 0, COLB), jax.random.fold_in(key_of[7], 1), 0, COLB - 1).astype(jnp.int32),
        "tile_count": draw_tile_count(jax.random.fold_in(key_of[9], 71), 0),
    }


def tile_sums(tile_bits, pick_blocks, place_blocks, is_live, source, out_blocks, transpose):
    edge = tile_bits.shape[-1]
    source_blocks = source.reshape(-1, edge, source.shape[-1]).astype(jnp.float32)
    chosen = jnp.take(source_blocks, pick_blocks, axis=0)
    bits = tile_bits.astype(jnp.float32)
    if transpose:
        products = jnp.einsum('kji,kjf->kif', bits, chosen, precision=lax.Precision.HIGHEST)
    else:
        products = jnp.einsum('kij,kjf->kif', bits, chosen, precision=lax.Precision.HIGHEST)
    targets = jnp.arange(out_blocks, dtype=jnp.int32)
    select = jnp.where((place_blocks[None, :] == targets[:, None]) & is_live[None, :], 1.0, 0.0).astype(jnp.float32)
    summed = jnp.einsum('bk,kif->bif', select, products, precision=lax.Precision.HIGHEST)
    return summed

def rounded(values):
    return lax.optimization_barrier(values.astype(jnp.bfloat16)).astype(jnp.float32)

def silu_pair(linear):
    sigma = jax.nn.sigmoid(linear)
    return (linear * sigma, sigma * (1.0 + linear * (1.0 - sigma)))

def reference(features, cotangent, self_weight, neigh_weight, degrees, adjacency, tile_rows, tile_cols, tile_count):
    device_count = N_ROW * N_COL
    tile_all = adjacency.reshape(device_count, K, BLK, BLK)
    rows_all = tile_rows.reshape(device_count, K)
    cols_all = tile_cols.reshape(device_count, K)
    count_all = tile_count.reshape(device_count)
    ranks = jnp.arange(device_count, dtype=jnp.int32)
    local_rows = jnp.arange(ROWB, dtype=jnp.int32)
    local_cols = jnp.arange(COLB, dtype=jnp.int32)
    slot_index = jnp.arange(K, dtype=jnp.int32)

    def row_owner(column):
        return ((local_rows // BPD * N_COL + column) * BPD + local_rows % BPD).astype(jnp.int32)

    def forward_step(carry, entry):
        tile_bits, row_ids, col_ids, count, rank = entry
        grid_row = rank // N_COL
        grid_col = rank % N_COL
        is_live = slot_index < count
        summed = tile_sums(tile_bits, grid_row * COLB + col_ids, row_ids, is_live, features, ROWB, False)
        return (carry.at[row_owner(grid_col)].add(rounded(summed)), None)
    start = jnp.zeros((NODES // BLK, BLK, F), jnp.float32)
    gathered, _ = lax.scan(forward_step, start, (tile_all, rows_all, cols_all, count_all, ranks))
    inverse = lax.rsqrt(jnp.maximum(degrees, 1).astype(jnp.float32))[:, None]
    mixed = (gathered.reshape(NODES, F) * inverse).astype(jnp.bfloat16)
    linear = jnp.dot(features, self_weight, preferred_element_type=jnp.float32) + jnp.dot(mixed, neigh_weight, preferred_element_type=jnp.float32)
    activated, slope = silu_pair(linear)
    hidden = activated.astype(jnp.bfloat16)
    grad_linear = (cotangent.astype(jnp.float32) * slope).astype(jnp.bfloat16)
    grad_mixed = (jnp.dot(grad_linear, neigh_weight.T, preferred_element_type=jnp.float32) * inverse).astype(jnp.bfloat16)

    def backward_step(carry, entry):
        tile_bits, row_ids, col_ids, count, rank = entry
        grid_row = rank // N_COL
        grid_col = rank % N_COL
        is_live = slot_index < count
        summed = tile_sums(tile_bits, row_owner(grid_col)[row_ids], col_ids, is_live, grad_mixed, COLB, True)
        return (carry.at[grid_row * COLB + local_cols].add(rounded(summed)), None)
    returned, _ = lax.scan(backward_step, start, (tile_all, rows_all, cols_all, count_all, ranks))
    grad_features = (jnp.dot(grad_linear, self_weight.T, preferred_element_type=jnp.float32) + returned.reshape(NODES, F)).astype(jnp.bfloat16)
    grad_self = jnp.einsum('nf,ng->fg', features.astype(jnp.float32), grad_linear.astype(jnp.float32), precision=lax.Precision.HIGHEST)
    grad_neigh = jnp.einsum('nf,ng->fg', mixed.astype(jnp.float32), grad_linear.astype(jnp.float32), precision=lax.Precision.HIGHEST)
    return (hidden, grad_features, grad_self, grad_neigh)
```

```python
import jax
import jax.numpy as jnp
from jax import lax
from jax.experimental import pallas as pl
from jax.experimental.pallas import tpu as pltpu
from jax.sharding import Mesh
from jax.sharding import PartitionSpec as P

NZ, NX, NY, NC = 8, 4, 8, 2
ALL = ("z", "x", "y", "core")
ROW = ("z", "x")
COL = ("y", "core")
B = 128
F = 128
GROUP = 8
WG = 16
BF = jnp.bfloat16
F32 = jnp.float32
VMEM = pl.BlockSpec(memory_space=pltpu.VMEM)
SMEM = pl.BlockSpec(memory_space=pltpu.SMEM)
PARAMS = pltpu.CompilerParams(vmem_limit_bytes=24 * 1024 * 1024)


def dot(a, b, contract=((1,), (0,))):
    return lax.dot_general(a, b, (contract, ((), ())), preferred_element_type=F32)


def split(value):
    high = value.astype(BF)
    low = (value - high.astype(F32)).astype(BF)
    return high, low


def joined(pair, rows):
    return pair[:rows].astype(F32) + pair[rows:].astype(F32)


def forward_kernel(rows, cols, count, tiles, source, partial, bits, acc):
    step = pl.program_id(0)
    last = pl.num_programs(0) - 1

    @pl.when(step == 0)
    def _():
        acc[...] = jnp.zeros_like(acc)

    products = []
    for i in range(GROUP):
        k = step * GROUP + i
        tile = tiles[i].astype(F32).astype(BF)
        bits[i] = tile
        products.append(dot(tile, source[cols[k]]))
    for i in range(GROUP):
        k = step * GROUP + i
        b = rows[k]
        place = jnp.where(k < count[0], (b % NX) * NZ + b // NX, NX * NZ)
        acc[place] += products[i]

    @pl.when(step == last)
    def _():
        partial[...] = acc[: NX * NZ].astype(BF)


def forward_sums(rows, cols, count, tiles, source):
    slots = tiles.shape[0]
    return pl.pallas_call(
        forward_kernel,
        grid=(slots // GROUP,),
        in_specs=[
            SMEM,
            SMEM,
            SMEM,
            pl.BlockSpec((GROUP, B, B), lambda i: (i, 0, 0)),
            pl.BlockSpec((NY * NC, B, F), lambda i: (0, 0, 0)),
        ],
        out_specs=[
            pl.BlockSpec((NX * NZ, B, F), lambda i: (0, 0, 0)),
            pl.BlockSpec((GROUP, B, B), lambda i: (i, 0, 0)),
        ],
        out_shape=[
            jax.ShapeDtypeStruct((NX * NZ, B, F), BF),
            jax.ShapeDtypeStruct((slots, B, B), BF),
        ],
        scratch_shapes=[pltpu.VMEM((NX * NZ + 1, B, F), F32)],
        compiler_params=PARAMS,
        name="forward_sums",
    )(rows, cols, count, tiles, source)


def dense_kernel(
    pieces, features, cotangent, self_weight, neigh_weight, inv_col, inv_row, hidden, base, payload
):
    total = pieces[0].astype(F32)
    for i in range(1, NZ):
        total += pieces[i].astype(F32)
    feats = features[...]
    mixed = (total * inv_col[...]).astype(BF)
    linear = dot(feats, self_weight[...]) + dot(mixed, neigh_weight[...])
    sigma = jax.nn.sigmoid(linear)
    hidden[...] = (linear * sigma).astype(BF)
    grad = (cotangent[...].astype(F32) * sigma * (1.0 + linear * (1.0 - sigma))).astype(BF)
    spread = (dot(neigh_weight[...], grad, ((1,), (1,))) * inv_row[...]).astype(BF)
    base[...] = dot(self_weight[...], grad, ((1,), (1,)))
    part = F // (NZ // 2)
    for i, left in enumerate((feats, mixed)):
        high, low = split(dot(left, grad, ((0,), (0,))))
        for j in range(NZ // 2):
            at = i * (NZ // 2) + j
            payload[at, pl.ds(0, B)] = spread
            payload[at, pl.ds(B, part)] = high[j * part : (j + 1) * part]
            payload[at, pl.ds(B + part, part)] = low[j * part : (j + 1) * part]


def dense_layer(pieces, features, cotangent, self_weight, neigh_weight, inv_col, inv_row):
    return pl.pallas_call(
        dense_kernel,
        in_specs=[VMEM] * 7,
        out_specs=[VMEM] * 3,
        out_shape=[
            jax.ShapeDtypeStruct((B, F), BF),
            jax.ShapeDtypeStruct((F, B), F32),
            jax.ShapeDtypeStruct((NZ, B + 64, F), BF),
        ],
        compiler_params=PARAMS,
        name="dense_layer",
    )(pieces, features, cotangent, self_weight, neigh_weight, inv_col, inv_row)


def relay_kernel(arrived, payload):
    for i in range(NZ):
        block = arrived[i, pl.ds(0, B)]
        for j in range(NX):
            payload[j, pl.ds(i * B, B)] = block
    total = joined(arrived[0, pl.ds(B, 64)], 32)
    for i in range(1, NZ):
        total += joined(arrived[i, pl.ds(B, 64)], 32)
    high, low = split(total)
    for j in range(NX):
        payload[j, pl.ds(NZ * B, WG)] = jnp.concatenate(
            [high[j * 8 : j * 8 + 8], low[j * 8 : j * 8 + 8]], 0
        )


def relay(arrived):
    return pl.pallas_call(
        relay_kernel,
        in_specs=[VMEM],
        out_specs=VMEM,
        out_shape=jax.ShapeDtypeStruct((NX, NZ * B + WG, F), BF),
        compiler_params=PARAMS,
        name="relay",
    )(arrived)


def backward_kernel(rows, cols, count, core, bits, spread, own, other, acc):
    acc[...] = jnp.zeros_like(acc)
    slots = bits.shape[0]

    def step(g, carry):
        products = []
        for i in range(GROUP):
            k = g * GROUP + i
            b = rows[k]
            source = spread[b % NX, pl.ds(pl.multiple_of((b // NX) * B, B), B)]
            products.append(dot(source, bits[k]))
        for i in range(GROUP):
            k = g * GROUP + i
            b = cols[k]
            place = jnp.where(k < count[0], (b % NC) * NY + b // NC, NY * NC)
            acc[place] += products[i]
        return carry

    lax.fori_loop(0, slots // GROUP, step, 0)
    me = core[0]
    for i in range(NY):
        own[pl.ds(i * B, B)] = acc[me * NY + i].astype(BF)
        other[pl.ds(i * B, B)] = acc[(1 - me) * NY + i].astype(BF)
    total = joined(spread[0, pl.ds(NZ * B, WG)], 8)
    for i in range(1, NX):
        total += joined(spread[i, pl.ds(NZ * B, WG)], 8)
    high, low = split(total)
    pair = jnp.concatenate([high, low], 0)
    own[pl.ds(NY * B, WG)] = pair
    other[pl.ds(NY * B, WG)] = pair


def backward_sums(rows, cols, count, core, bits, spread):
    return pl.pallas_call(
        backward_kernel,
        in_specs=[SMEM, SMEM, SMEM, SMEM, VMEM, VMEM],
        out_specs=[VMEM, VMEM],
        out_shape=[jax.ShapeDtypeStruct((NY * B + WG, B), BF)] * 2,
        scratch_shapes=[pltpu.VMEM((NY * NC + 1, F, B), F32)],
        compiler_params=PARAMS,
        name="backward_sums",
    )(rows, cols, count, core, bits, spread)


def merge_kernel(own, other, payload):
    pair = joined(own[pl.ds(NY * B, WG)], 8) + joined(other[pl.ds(NY * B, WG)], 8)
    high, low = split(pair)
    tail = jnp.concatenate([high, low], 0)
    for i in range(NY):
        at = pl.ds(i * B, B)
        payload[i, pl.ds(0, B)] = (own[at].astype(F32) + other[at].astype(F32)).astype(BF)
        payload[i, pl.ds(B, WG)] = tail


def merge(own, other):
    return pl.pallas_call(
        merge_kernel,
        in_specs=[VMEM, VMEM],
        out_specs=VMEM,
        out_shape=jax.ShapeDtypeStruct((NY, B + WG, B), BF),
        compiler_params=PARAMS,
        name="merge",
    )(own, other)


def final_kernel(arrived, base, grad_features, chunk):
    total = base[...]
    tail = joined(arrived[0, pl.ds(B, WG)], 8)
    for i in range(NY):
        total += arrived[i, pl.ds(0, B)].astype(F32)
        if i > 0:
            tail += joined(arrived[i, pl.ds(B, WG)], 8)
    grad_features[...] = total.T.astype(BF)
    for i in range(NZ * NX):
        chunk[i] = tail


def final(arrived, base):
    return pl.pallas_call(
        final_kernel,
        in_specs=[VMEM, VMEM],
        out_specs=[VMEM, VMEM],
        out_shape=[
            jax.ShapeDtypeStruct((B, F), BF),
            jax.ShapeDtypeStruct((NZ * NX, 8, F), F32),
        ],
        compiler_params=PARAMS,
        name="final",
    )(arrived, base)


def exchange(value, axis):
    return lax.all_to_all(value, axis, 0, 0, tiled=True)


def body(
    features,
    cotangent,
    self_weight,
    neigh_weight,
    degrees,
    adjacency,
    tile_rows,
    tile_cols,
    tile_count,
):
    slots = adjacency.shape[2]
    tiles = adjacency.reshape(slots, B, B)
    rows = tile_rows.reshape(slots)
    cols = tile_cols.reshape(slots)
    count = tile_count.reshape(1)
    core = lax.axis_index("core").reshape(1)
    inverse = lax.rsqrt(jnp.maximum(degrees, 1).astype(F32))

    source = lax.all_gather(features, COL, axis=0, tiled=False)
    partial, bits = forward_sums(rows, cols, count, tiles, source)
    arrived = exchange(partial.reshape(NX, NZ * B, F), "x")
    summed = jnp.sum(arrived, axis=0, dtype=F32).astype(BF)
    pieces = exchange(summed.reshape(NZ, B, F), "z")
    hidden, base, payload = dense_layer(
        pieces, features, cotangent, self_weight, neigh_weight, inverse[:, None], inverse[None, :]
    )
    spread = exchange(relay(exchange(payload, "z")), "x")
    own, other = backward_sums(rows, cols, count, core, bits, spread)
    other = lax.ppermute(other, "core", [(0, 1), (1, 0)])
    returned = exchange(merge(own, other), "y")
    grad_features, chunk = final(returned, base)
    grads = exchange(chunk, ROW).reshape(2, F, F)
    return (hidden, grad_features, grads[0], grads[1])


def solution(mesh):
    grid = Mesh(mesh.devices.reshape(NZ, NX, NY, NC), ALL)
    in_specs = (
        P(ALL, None),
        P(ALL, None),
        P(),
        P(),
        P(ALL),
        P(ROW, COL, None, None, None),
        P(ROW, COL, None),
        P(ROW, COL, None),
        P(ROW, COL),
    )
    out_specs = (P(ALL, None), P(ALL, None), P(), P())
    return jax.shard_map(body, mesh=grid, in_specs=in_specs, out_specs=out_specs, check_vma=False)
```

```python
import jax
import jax.numpy as jnp
from jax import lax
from jax.experimental import pallas as pl
from jax.experimental.pallas import tpu as pltpu
from jax.sharding import Mesh
from jax.sharding import PartitionSpec as P

NZ, NX, NY, NC = 8, 4, 8, 2
ALL = ("z", "x", "y", "core")
ROW = ("z", "x")
COL = ("y", "core")
B = 128
F = 128
WG = 32
BF = jnp.bfloat16
F32 = jnp.float32


def cost(us):
    return pl.CostEstimate(flops=0, bytes_accessed=int(us * 3.69e6), transcendentals=0)


VMEM = pl.BlockSpec(memory_space=pltpu.VMEM)
SMEM = pl.BlockSpec(memory_space=pltpu.SMEM)
PARAMS = pltpu.CompilerParams(vmem_limit_bytes=24 * 1024 * 1024)


def dot(a, b, contract=((1,), (0,))):
    return lax.dot_general(a, b, (contract, ((), ())), preferred_element_type=F32)


def forward_kernel(plan, bits, source, partial, acc):
    acc[...] = jnp.zeros_like(acc)

    slots = bits.shape[0]
    products = [dot(bits[k], source[plan[0, k]]) for k in range(slots)]
    for k in range(slots):
        acc[plan[3, k]] += products[k]
    partial[...] = acc[: NX * NZ].astype(BF)


def forward_sums(plan, bits, source):
    return pl.pallas_call(
        forward_kernel,
        in_specs=[SMEM, VMEM, VMEM],
        out_specs=VMEM,
        out_shape=jax.ShapeDtypeStruct((NX * NZ, B, F), BF),
        scratch_shapes=[pltpu.VMEM((NX * NZ + 1, B, F), F32)],
        compiler_params=PARAMS,
        cost_estimate=cost(2.7),
        name="forward_sums",
    )(plan, bits, source)


def add_kernel(arrived, summed):
    total = arrived[0].astype(F32)
    for i in range(1, arrived.shape[0]):
        total += arrived[i].astype(F32)
    summed[...] = total.astype(BF)


def add_pieces(arrived):
    return pl.pallas_call(
        add_kernel,
        in_specs=[VMEM],
        out_specs=VMEM,
        out_shape=jax.ShapeDtypeStruct(arrived.shape[1:], BF),
        compiler_params=PARAMS,
        cost_estimate=cost(0.8),
        name="add_pieces",
    )(arrived)


def dense_kernel(
    pieces,
    features,
    cotangent,
    self_weight,
    neigh_weight,
    degrees,
    hidden,
    base,
    payload,
):
    total = pieces[0].astype(F32)
    for i in range(1, NZ):
        total += pieces[i].astype(F32)
    feats = features[...]
    inverse = lax.rsqrt(jnp.maximum(degrees[...], 1).astype(F32))
    mixed = (total * jnp.broadcast_to(inverse, (B, B)).T).astype(BF)
    linear = dot(feats, self_weight[...]) + dot(mixed, neigh_weight[...])
    sigma = jax.nn.sigmoid(linear)
    hidden[...] = (linear * sigma).astype(BF)
    grad = (cotangent[...].astype(F32) * sigma * (1.0 + linear * (1.0 - sigma))).astype(BF)
    spread = (dot(neigh_weight[...], grad, ((1,), (1,))) * inverse).astype(BF)
    base[...] = dot(self_weight[...], grad, ((1,), (1,)))
    for i, left in enumerate((feats, mixed)):
        value = dot(left, grad, ((0,), (0,))).astype(BF)
        for j in range(NZ // 2):
            at = i * (NZ // 2) + j
            payload[at, pl.ds(0, B)] = spread
            payload[at, pl.ds(B, WG)] = value[j * WG : (j + 1) * WG]


def dense_layer(pieces, features, cotangent, self_weight, neigh_weight, degrees):
    return pl.pallas_call(
        dense_kernel,
        in_specs=[VMEM] * 6,
        out_specs=[VMEM] * 3,
        out_shape=[
            jax.ShapeDtypeStruct((B, F), BF),
            jax.ShapeDtypeStruct((F, B), F32),
            jax.ShapeDtypeStruct((NZ, F + WG, B), BF),
        ],
        compiler_params=PARAMS,
        cost_estimate=cost(1.1),
        name="dense_layer",
    )(pieces, features, cotangent, self_weight, neigh_weight, degrees)


def relay_kernel(arrived, payload):
    total = arrived[0, pl.ds(F, WG)].astype(F32)
    for i in range(1, NZ):
        total += arrived[i, pl.ds(F, WG)].astype(F32)
    chunk = total.astype(BF)
    for j in range(NX):
        for i in range(NZ):
            payload[j, pl.ds(i * F, F)] = arrived[i, pl.ds(0, F)]
        payload[j, pl.ds(NZ * F, WG)] = chunk


def relay(arrived):
    return pl.pallas_call(
        relay_kernel,
        in_specs=[VMEM],
        out_specs=VMEM,
        out_shape=jax.ShapeDtypeStruct((NX, NZ * F + WG, B), BF),
        compiler_params=PARAMS,
        cost_estimate=cost(1.0),
        name="relay",
    )(arrived)


def backward_kernel(plan, bits, spread, own, other, acc):
    acc[...] = jnp.zeros_like(acc)

    slots = bits.shape[0]
    products = []
    for k in range(slots):
        at = plan[1, k]
        block = spread[at // NZ, pl.ds(pl.multiple_of(at % NZ * F, F), F)]
        products.append(dot(block, bits[k]))
    for k in range(slots):
        acc[plan[2, k]] += products[k]
    total = spread[0, pl.ds(NZ * F, WG)].astype(F32)
    for i in range(1, NX):
        total += spread[i, pl.ds(NZ * F, WG)].astype(F32)
    chunk = total.astype(BF)
    me = plan[4, 0]
    for i in range(NY):
        own[pl.ds(i * F, F)] = acc[me * NY + i].astype(BF)
        other[pl.ds(i * F, F)] = acc[(1 - me) * NY + i].astype(BF)
    own[pl.ds(NY * F, WG)] = chunk
    other[pl.ds(NY * F, WG)] = chunk


def backward_sums(plan, bits, spread):
    return pl.pallas_call(
        backward_kernel,
        in_specs=[SMEM, VMEM, VMEM],
        out_specs=[VMEM, VMEM],
        out_shape=[jax.ShapeDtypeStruct((NY * F + WG, B), BF)] * 2,
        scratch_shapes=[pltpu.VMEM((NY * NC + 1, F, B), F32)],
        compiler_params=PARAMS,
        cost_estimate=cost(2.6),
        name="backward_sums",
    )(plan, bits, spread)


def merge_kernel(core, own, other, payload):
    them = 1 - core[0]
    tail = own[pl.ds(NY * F, WG)].astype(F32) + other[them, pl.ds(NY * F, WG)].astype(F32)
    for i in range(NY):
        at = pl.ds(i * F, F)
        payload[i, pl.ds(0, F)] = (own[at].astype(F32) + other[them, at].astype(F32)).astype(BF)
        payload[i, pl.ds(F, WG)] = tail.astype(BF)


def merge(core, own, other):
    return pl.pallas_call(
        merge_kernel,
        in_specs=[SMEM, VMEM, VMEM],
        out_specs=VMEM,
        out_shape=jax.ShapeDtypeStruct((NY, F + WG, B), BF),
        compiler_params=PARAMS,
        cost_estimate=cost(0.5),
        name="merge",
    )(core, own, other)


def final_kernel(arrived, base, grad_features, chunk):
    total = base[...]
    tail = arrived[0, pl.ds(F, WG)].astype(F32)
    for i in range(NY):
        total += arrived[i, pl.ds(0, F)].astype(F32)
        if i > 0:
            tail += arrived[i, pl.ds(F, WG)].astype(F32)
    grad_features[...] = total.T.astype(BF)
    for i in range(NZ):
        chunk[i] = tail.astype(BF)


def final(arrived, base):
    return pl.pallas_call(
        final_kernel,
        in_specs=[VMEM, VMEM],
        out_specs=[VMEM, VMEM],
        out_shape=[
            jax.ShapeDtypeStruct((B, F), BF),
            jax.ShapeDtypeStruct((NZ, WG, F), BF),
        ],
        compiler_params=PARAMS,
        cost_estimate=cost(0.8),
        name="final",
    )(arrived, base)


def exchange(value, axis):
    return lax.all_to_all(value, axis, 0, 0, tiled=True)


def body(
    features,
    cotangent,
    self_weight,
    neigh_weight,
    degrees,
    adjacency,
    tile_rows,
    tile_cols,
    tile_count,
):
    slots = adjacency.shape[2]
    rows = tile_rows.reshape(slots)
    cols = tile_cols.reshape(slots)
    core = lax.axis_index("core")
    slot = jnp.arange(slots, dtype=jnp.int32)
    live = slot < tile_count.reshape(())
    col_at = cols % NC * NY + cols // NC
    row_at = rows % NX * NZ + rows // NX
    plan = jnp.stack(
        [
            col_at,
            row_at,
            jnp.where(live, col_at, NY * NC),
            jnp.where(live, row_at, NX * NZ),
            jnp.full_like(slot, core),
        ]
    )
    bits = adjacency.reshape(slots, B, B).astype(BF)

    near = exchange(jnp.broadcast_to(features, (NY, B, F)), "y")
    source = lax.all_gather(near, "core", axis=0, tiled=True)
    partial = forward_sums(plan, bits, source)
    arrived = exchange(partial.reshape(NX, NZ, B, F), "x")
    pieces = exchange(add_pieces(arrived), "z")
    hidden, base, payload = dense_layer(
        pieces, features, cotangent, self_weight, neigh_weight, degrees.reshape(1, B)
    )
    spread = exchange(relay(exchange(payload, "z")), "x")
    own, other = backward_sums(plan, bits, spread)
    other = lax.all_gather(other, "core", axis=0, tiled=False)
    returned = exchange(merge(core.reshape(1), own, other), "y")
    grad_features, chunk = final(returned, base)
    grads = exchange(chunk, "z").reshape(2, F, F).astype(F32)
    return (hidden, grad_features, grads[0], grads[1])


def solution(mesh):
    grid = Mesh(mesh.devices.reshape(NZ, NX, NY, NC), ALL)
    in_specs = (
        P(ALL, None),
        P(ALL, None),
        P(),
        P(),
        P(ALL),
        P(ROW, COL, None, None, None),
        P(ROW, COL, None),
        P(ROW, COL, None),
        P(ROW, COL),
    )
    out_specs = (P(ALL, None), P(ALL, None), P(), P())
    return jax.shard_map(body, mesh=grid, in_specs=in_specs, out_specs=out_specs, check_vma=False)
```

```python
import jax
import jax.numpy as jnp
from jax import lax
from jax.experimental import pallas as pl
from jax.experimental.pallas import tpu as pltpu
from jax.sharding import Mesh
from jax.sharding import PartitionSpec as P

NZ, NX, NY, NC = 8, 4, 8, 2
ALL = ("z", "x", "y", "core")
ROW = ("z", "x")
COL = ("y", "core")
B = 128
F = 128
WG = 32
BF = jnp.bfloat16
F32 = jnp.float32


def cost(us):
    return pl.CostEstimate(flops=0, bytes_accessed=int(us * 3.69e6), transcendentals=0)


VMEM = pl.BlockSpec(memory_space=pltpu.VMEM)
SMEM = pl.BlockSpec(memory_space=pltpu.SMEM)
PARAMS = pltpu.CompilerParams(vmem_limit_bytes=24 * 1024 * 1024)


def dot(a, b, contract=((1,), (0,))):
    return lax.dot_general(a, b, (contract, ((), ())), preferred_element_type=F32)


def forward_kernel(plan, bits, source, partial, acc):
    acc[...] = jnp.zeros_like(acc)

    slots = bits.shape[0]
    products = [dot(bits[k], source[plan[0, k]]) for k in range(slots)]
    for k in range(slots):
        acc[plan[3, k]] += products[k]
    partial[...] = acc[: NX * NZ].astype(BF)


def forward_sums(plan, bits, source):
    return pl.pallas_call(
        forward_kernel,
        in_specs=[SMEM, VMEM, VMEM],
        out_specs=VMEM,
        out_shape=jax.ShapeDtypeStruct((NX * NZ, B, F), BF),
        scratch_shapes=[pltpu.VMEM((NX * NZ + 1, B, F), F32)],
        compiler_params=PARAMS,
        cost_estimate=cost(2.7),
        name="forward_sums",
    )(plan, bits, source)


def add_kernel(arrived, summed):
    total = arrived[0].astype(F32)
    for i in range(1, arrived.shape[0]):
        total += arrived[i].astype(F32)
    summed[...] = total.astype(BF)


def add_pieces(arrived):
    return pl.pallas_call(
        add_kernel,
        in_specs=[VMEM],
        out_specs=VMEM,
        out_shape=jax.ShapeDtypeStruct(arrived.shape[1:], BF),
        compiler_params=PARAMS,
        cost_estimate=cost(0.8),
        name="add_pieces",
    )(arrived)


def dense_kernel(
    pieces,
    features,
    cotangent,
    self_weight,
    neigh_weight,
    degrees,
    hidden,
    base,
    column,
    grads,
):
    total = pieces[0].astype(F32)
    for i in range(1, NZ):
        total += pieces[i].astype(F32)
    feats = features[...]
    inverse = lax.rsqrt(jnp.maximum(degrees[...], 1).astype(F32))
    mixed = (total * jnp.broadcast_to(inverse, (B, B)).T).astype(BF)
    linear = dot(feats, self_weight[...]) + dot(mixed, neigh_weight[...])
    sigma = jax.nn.sigmoid(linear)
    hidden[...] = (linear * sigma).astype(BF)
    grad = (cotangent[...].astype(F32) * sigma * (1.0 + linear * (1.0 - sigma))).astype(BF)
    spread = (dot(neigh_weight[...], grad, ((1,), (1,))) * inverse).astype(BF)
    base[...] = dot(self_weight[...], grad, ((1,), (1,)))
    column[...] = spread
    for i, left in enumerate((feats, mixed)):
        value = dot(left, grad, ((0,), (0,))).astype(BF)
        for j in range(NY // 2):
            grads[i * (NY // 2) + j] = value[j * WG : (j + 1) * WG]


def dense_layer(pieces, features, cotangent, self_weight, neigh_weight, degrees):
    return pl.pallas_call(
        dense_kernel,
        in_specs=[VMEM] * 6,
        out_specs=[VMEM] * 4,
        out_shape=[
            jax.ShapeDtypeStruct((B, F), BF),
            jax.ShapeDtypeStruct((F, B), F32),
            jax.ShapeDtypeStruct((F, B), BF),
            jax.ShapeDtypeStruct((NY, WG, F), BF),
        ],
        compiler_params=PARAMS,
        cost_estimate=cost(1.1),
        name="dense_layer",
    )(pieces, features, cotangent, self_weight, neigh_weight, degrees)


def pack_kernel(column, grads, payload):
    total = grads[0].astype(F32)
    for i in range(1, NY):
        total += grads[i].astype(F32)
    chunk = total.astype(BF)
    for i in range(NZ):
        payload[i, pl.ds(0, F)] = column[...]
        payload[i, pl.ds(F, WG)] = chunk


def pack(column, grads):
    return pl.pallas_call(
        pack_kernel,
        in_specs=[VMEM, VMEM],
        out_specs=VMEM,
        out_shape=jax.ShapeDtypeStruct((NZ, F + WG, B), BF),
        compiler_params=PARAMS,
        cost_estimate=cost(0.3),
        name="pack",
    )(column, grads)


def relay_kernel(arrived, payload):
    total = arrived[0, pl.ds(F, WG)].astype(F32)
    for i in range(1, NZ):
        total += arrived[i, pl.ds(F, WG)].astype(F32)
    chunk = total.astype(BF)
    for j in range(NX):
        for i in range(NZ):
            payload[j, pl.ds(i * F, F)] = arrived[i, pl.ds(0, F)]
        payload[j, pl.ds(NZ * F, WG)] = chunk


def relay(arrived):
    return pl.pallas_call(
        relay_kernel,
        in_specs=[VMEM],
        out_specs=VMEM,
        out_shape=jax.ShapeDtypeStruct((NX, NZ * F + WG, B), BF),
        compiler_params=PARAMS,
        cost_estimate=cost(1.0),
        name="relay",
    )(arrived)


def backward_kernel(plan, bits, spread, payload, acc):
    acc[...] = jnp.zeros_like(acc)

    slots = bits.shape[0]
    products = []
    for k in range(slots):
        at = plan[1, k]
        block = spread[at // NZ, pl.ds(pl.multiple_of(at % NZ * F, F), F)]
        products.append(dot(block, bits[k]))
    for k in range(slots):
        acc[plan[2, k]] += products[k]
    tail = spread[0, pl.ds(NZ * F, WG)].astype(F32)
    for i in range(1, NX):
        tail += spread[i, pl.ds(NZ * F, WG)].astype(F32)
    for i in range(NY):
        for j in range(NC):
            payload[i, pl.ds(j * F, F)] = acc[j * NY + i].astype(BF)
        payload[i, pl.ds(NC * F, WG)] = tail.astype(BF)


def backward_sums(plan, bits, spread):
    return pl.pallas_call(
        backward_kernel,
        in_specs=[SMEM, VMEM, VMEM],
        out_specs=VMEM,
        out_shape=jax.ShapeDtypeStruct((NY, NC * F + WG, B), BF),
        scratch_shapes=[pltpu.VMEM((NY * NC + 1, F, B), F32)],
        compiler_params=PARAMS,
        cost_estimate=cost(1.5),
        name="backward_sums",
    )(plan, bits, spread)


def collect_kernel(arrived, sums):
    total = arrived[0, pl.ds(0, NC * F)].astype(F32)
    for i in range(1, NY):
        total += arrived[i, pl.ds(0, NC * F)].astype(F32)
    sums[pl.ds(0, NC * F)] = total.astype(BF)
    for i in range(NY):
        sums[pl.ds(NC * F + i * WG, WG)] = arrived[i, pl.ds(NC * F, WG)]


def collect(arrived):
    return pl.pallas_call(
        collect_kernel,
        in_specs=[VMEM],
        out_specs=VMEM,
        out_shape=jax.ShapeDtypeStruct((2 * NC * F, B), BF),
        compiler_params=PARAMS,
        cost_estimate=cost(0.3),
        name="collect",
    )(arrived)


def final_kernel(core, both, base, grad_features, grad_self, grad_neigh):
    mine = pl.ds(pl.multiple_of(core[0] * F, F), F)
    total = base[...] + (both[0, mine].astype(F32) + both[1, mine].astype(F32))
    grad_features[...] = total.T.astype(BF)
    for i, out in ((NC, grad_self), (NC + 1, grad_neigh)):
        rows = pl.ds(i * F, F)
        out[...] = both[0, rows].astype(F32) + both[1, rows].astype(F32)


def final(core, both, base):
    return pl.pallas_call(
        final_kernel,
        in_specs=[SMEM, VMEM, VMEM],
        out_specs=[VMEM] * 3,
        out_shape=[
            jax.ShapeDtypeStruct((B, F), BF),
            jax.ShapeDtypeStruct((F, F), F32),
            jax.ShapeDtypeStruct((F, F), F32),
        ],
        compiler_params=PARAMS,
        cost_estimate=cost(0.8),
        name="final",
    )(core, both, base)


def exchange(value, axis):
    return lax.all_to_all(value, axis, 0, 0, tiled=True)


def body(
    features,
    cotangent,
    self_weight,
    neigh_weight,
    degrees,
    adjacency,
    tile_rows,
    tile_cols,
    tile_count,
):
    slots = adjacency.shape[2]
    rows = tile_rows.reshape(slots)
    cols = tile_cols.reshape(slots)
    core = lax.axis_index("core")
    slot = jnp.arange(slots, dtype=jnp.int32)
    live = slot < tile_count.reshape(())
    col_at = cols % NC * NY + cols // NC
    row_at = rows % NX * NZ + rows // NX
    plan = jnp.stack(
        [
            col_at,
            row_at,
            jnp.where(live, col_at, NY * NC),
            jnp.where(live, row_at, NX * NZ),
            jnp.full_like(slot, core),
        ]
    )
    bits = adjacency.reshape(slots, B, B).astype(BF)

    near = exchange(jnp.broadcast_to(features, (NY, B, F)), "y")
    source = lax.all_gather(near, "core", axis=0, tiled=True)
    partial = forward_sums(plan, bits, source)
    arrived = exchange(partial.reshape(NX, NZ, B, F), "x")
    pieces = exchange(add_pieces(arrived), "z")
    hidden, base, column, grads = dense_layer(
        pieces, features, cotangent, self_weight, neigh_weight, degrees.reshape(1, B)
    )
    payload = pack(column, exchange(grads, "y"))
    spread = exchange(relay(exchange(payload, "z")), "x")
    returned = exchange(backward_sums(plan, bits, spread), "y")
    both = lax.all_gather(collect(returned), "core", axis=0, tiled=False)
    return (hidden, *final(core.reshape(1), both, base))


def solution(mesh):
    grid = Mesh(mesh.devices.reshape(NZ, NX, NY, NC), ALL)
    in_specs = (
        P(ALL, None),
        P(ALL, None),
        P(),
        P(),
        P(ALL),
        P(ROW, COL, None, None, None),
        P(ROW, COL, None),
        P(ROW, COL, None),
        P(ROW, COL),
    )
    out_specs = (P(ALL, None), P(ALL, None), P(), P())
    return jax.shard_map(body, mesh=grid, in_specs=in_specs, out_specs=out_specs, check_vma=False)
```

```python
import jax
import jax.numpy as jnp
from jax import lax
from jax.experimental import pallas as pl
from jax.experimental.pallas import tpu as pltpu
from jax.sharding import Mesh
from jax.sharding import PartitionSpec as P

NZ, NX, NY, NC = 8, 4, 8, 2
ALL = ("z", "x", "y", "core")
ROW = ("z", "x")
COL = ("y", "core")
B = 128
F = 128
WG = 32
BF = jnp.bfloat16
F32 = jnp.float32


def cost(us):
    return pl.CostEstimate(flops=0, bytes_accessed=int(us * 3.69e6), transcendentals=0)


VMEM = pl.BlockSpec(memory_space=pltpu.VMEM)
ANY = pl.BlockSpec(memory_space=pl.ANY)
SMEM = pl.BlockSpec(memory_space=pltpu.SMEM)
PARAMS = pltpu.CompilerParams(vmem_limit_bytes=24 * 1024 * 1024)


def dot(a, b, contract=((1,), (0,))):
    return lax.dot_general(a, b, (contract, ((), ())), preferred_element_type=F32)


def forward_kernel(whole, bits, source, partial, acc, plan, sem):
    copy = pltpu.make_async_copy(whole, plan, sem)
    copy.start()
    acc[...] = jnp.zeros_like(acc)
    copy.wait()

    slots = bits.shape[0]
    products = [dot(bits[k], source[plan[0, k]]) for k in range(slots)]
    for k in range(slots):
        acc[plan[3, k]] += products[k]
    partial[...] = acc[: NX * NZ].astype(BF)


def forward_sums(plan, bits, source):
    return pl.pallas_call(
        forward_kernel,
        in_specs=[ANY, VMEM, VMEM],
        out_specs=VMEM,
        out_shape=jax.ShapeDtypeStruct((NX * NZ, B, F), BF),
        scratch_shapes=[
            pltpu.VMEM((NX * NZ + 1, B, F), F32),
            pltpu.SMEM(plan.shape, jnp.int32),
            pltpu.SemaphoreType.DMA,
        ],
        compiler_params=PARAMS,
        cost_estimate=cost(2.7),
        name="forward_sums",
    )(plan, bits, source)


def add_kernel(arrived, summed):
    total = arrived[0].astype(F32)
    for i in range(1, arrived.shape[0]):
        total += arrived[i].astype(F32)
    summed[...] = total.astype(BF)


def add_pieces(arrived):
    return pl.pallas_call(
        add_kernel,
        in_specs=[VMEM],
        out_specs=VMEM,
        out_shape=jax.ShapeDtypeStruct(arrived.shape[1:], BF),
        compiler_params=PARAMS,
        cost_estimate=cost(0.8),
        name="add_pieces",
    )(arrived)


def dense_kernel(
    pieces,
    features,
    cotangent,
    self_weight,
    neigh_weight,
    degrees,
    hidden,
    base,
    column,
    grads,
):
    total = pieces[0].astype(F32)
    for i in range(1, NZ):
        total += pieces[i].astype(F32)
    feats = features[...]
    inverse = lax.rsqrt(jnp.maximum(degrees[...], 1).astype(F32))
    mixed = (total * jnp.broadcast_to(inverse, (B, B)).T).astype(BF)
    linear = dot(feats, self_weight[...]) + dot(mixed, neigh_weight[...])
    sigma = jax.nn.sigmoid(linear)
    hidden[...] = (linear * sigma).astype(BF)
    grad = (cotangent[...].astype(F32) * sigma * (1.0 + linear * (1.0 - sigma))).astype(BF)
    spread = (dot(neigh_weight[...], grad, ((1,), (1,))) * inverse).astype(BF)
    base[...] = dot(self_weight[...], grad, ((1,), (1,)))
    column[...] = spread
    for i, left in enumerate((feats, mixed)):
        value = dot(left, grad, ((0,), (0,))).astype(BF)
        for j in range(NY // 2):
            grads[i * (NY // 2) + j] = value[j * WG : (j + 1) * WG]


def dense_layer(pieces, features, cotangent, self_weight, neigh_weight, degrees):
    return pl.pallas_call(
        dense_kernel,
        in_specs=[VMEM] * 6,
        out_specs=[VMEM] * 4,
        out_shape=[
            jax.ShapeDtypeStruct((B, F), BF),
            jax.ShapeDtypeStruct((F, B), F32),
            jax.ShapeDtypeStruct((F, B), BF),
            jax.ShapeDtypeStruct((NY, WG, F), BF),
        ],
        compiler_params=PARAMS,
        cost_estimate=cost(1.1),
        name="dense_layer",
    )(pieces, features, cotangent, self_weight, neigh_weight, degrees)


def pack_kernel(column, grads, payload):
    total = grads[0].astype(F32)
    for i in range(1, NY):
        total += grads[i].astype(F32)
    chunk = total.astype(BF)
    for i in range(NZ):
        payload[i, pl.ds(0, F)] = column[...]
        payload[i, pl.ds(F, WG)] = chunk


def pack(column, grads):
    return pl.pallas_call(
        pack_kernel,
        in_specs=[VMEM, VMEM],
        out_specs=VMEM,
        out_shape=jax.ShapeDtypeStruct((NZ, F + WG, B), BF),
        compiler_params=PARAMS,
        cost_estimate=cost(0.3),
        name="pack",
    )(column, grads)


def relay_kernel(arrived, payload):
    total = arrived[0, pl.ds(F, WG)].astype(F32)
    for i in range(1, NZ):
        total += arrived[i, pl.ds(F, WG)].astype(F32)
    chunk = total.astype(BF)
    for j in range(NX):
        for i in range(NZ):
            payload[j, pl.ds(i * F, F)] = arrived[i, pl.ds(0, F)]
        payload[j, pl.ds(NZ * F, WG)] = chunk


def relay(arrived):
    return pl.pallas_call(
        relay_kernel,
        in_specs=[VMEM],
        out_specs=VMEM,
        out_shape=jax.ShapeDtypeStruct((NX, NZ * F + WG, B), BF),
        compiler_params=PARAMS,
        cost_estimate=cost(1.0),
        name="relay",
    )(arrived)


def backward_kernel(whole, bits, spread, payload, acc, plan, sem):
    copy = pltpu.make_async_copy(whole, plan, sem)
    copy.start()
    acc[...] = jnp.zeros_like(acc)
    copy.wait()

    slots = bits.shape[0]
    products = []
    for k in range(slots):
        at = plan[1, k]
        block = spread[at // NZ, pl.ds(pl.multiple_of(at % NZ * F, F), F)]
        products.append(dot(block, bits[k]))
    for k in range(slots):
        acc[plan[2, k]] += products[k]
    tail = spread[0, pl.ds(NZ * F, WG)].astype(F32)
    for i in range(1, NX):
        tail += spread[i, pl.ds(NZ * F, WG)].astype(F32)
    for i in range(NY):
        for j in range(NC):
            payload[i, pl.ds(j * F, F)] = acc[j * NY + i].astype(BF)
        payload[i, pl.ds(NC * F, WG)] = tail.astype(BF)


def backward_sums(plan, bits, spread):
    return pl.pallas_call(
        backward_kernel,
        in_specs=[ANY, VMEM, VMEM],
        out_specs=VMEM,
        out_shape=jax.ShapeDtypeStruct((NY, NC * F + WG, B), BF),
        scratch_shapes=[
            pltpu.VMEM((NY * NC + 1, F, B), F32),
            pltpu.SMEM(plan.shape, jnp.int32),
            pltpu.SemaphoreType.DMA,
        ],
        compiler_params=PARAMS,
        cost_estimate=cost(1.5),
        name="backward_sums",
    )(plan, bits, spread)


def collect_kernel(arrived, sums):
    total = arrived[0, pl.ds(0, NC * F)].astype(F32)
    for i in range(1, NY):
        total += arrived[i, pl.ds(0, NC * F)].astype(F32)
    sums[pl.ds(0, NC * F)] = total.astype(BF)
    for i in range(NY):
        sums[pl.ds(NC * F + i * WG, WG)] = arrived[i, pl.ds(NC * F, WG)]


def collect(arrived):
    return pl.pallas_call(
        collect_kernel,
        in_specs=[VMEM],
        out_specs=VMEM,
        out_shape=jax.ShapeDtypeStruct((2 * NC * F, B), BF),
        compiler_params=PARAMS,
        cost_estimate=cost(0.3),
        name="collect",
    )(arrived)


def final_kernel(core, both, base, activated, hidden, grad_features, grad_self, grad_neigh):
    hidden[...] = activated[...]
    mine = pl.ds(pl.multiple_of(core[0] * F, F), F)
    total = base[...] + (both[0, mine].astype(F32) + both[1, mine].astype(F32))
    grad_features[...] = total.T.astype(BF)
    for i, out in ((NC, grad_self), (NC + 1, grad_neigh)):
        rows = pl.ds(i * F, F)
        out[...] = both[0, rows].astype(F32) + both[1, rows].astype(F32)


def final(core, both, base, activated):
    return pl.pallas_call(
        final_kernel,
        in_specs=[SMEM, VMEM, VMEM, VMEM],
        out_specs=[VMEM] * 4,
        out_shape=[
            jax.ShapeDtypeStruct((B, F), BF),
            jax.ShapeDtypeStruct((B, F), BF),
            jax.ShapeDtypeStruct((F, F), F32),
            jax.ShapeDtypeStruct((F, F), F32),
        ],
        compiler_params=PARAMS,
        cost_estimate=cost(0.8),
        name="final",
    )(core, both, base, activated)


def exchange(value, axis):
    return lax.all_to_all(value, axis, 0, 0, tiled=True)


def body(
    features,
    cotangent,
    self_weight,
    neigh_weight,
    degrees,
    adjacency,
    tile_rows,
    tile_cols,
    tile_count,
):
    slots = adjacency.shape[2]
    rows = tile_rows.reshape(slots)
    cols = tile_cols.reshape(slots)
    core = lax.axis_index("core")
    slot = jnp.arange(slots, dtype=jnp.int32)
    live = slot < tile_count.reshape(())
    col_at = cols % NC * NY + cols // NC
    row_at = rows % NX * NZ + rows // NX
    plan = jnp.stack(
        [
            col_at,
            row_at,
            jnp.where(live, col_at, NY * NC),
            jnp.where(live, row_at, NX * NZ),
            jnp.full_like(slot, core),
        ]
    )
    bits = adjacency.reshape(slots, B, B).astype(BF)

    near = exchange(jnp.broadcast_to(features, (NY, B, F)), "y")
    source = lax.all_gather(near, "core", axis=0, tiled=True)
    partial = forward_sums(plan, bits, source)
    arrived = exchange(partial.reshape(NX, NZ, B, F), "x")
    pieces = exchange(add_pieces(arrived), "z")
    activated, base, column, grads = dense_layer(
        pieces, features, cotangent, self_weight, neigh_weight, degrees.reshape(1, B)
    )
    payload = pack(column, exchange(grads, "y"))
    spread = exchange(relay(exchange(payload, "z")), "x")
    returned = exchange(backward_sums(plan, bits, spread), "y")
    both = lax.all_gather(collect(returned), "core", axis=0, tiled=False)
    return tuple(final(core.reshape(1), both, base, activated))


def solution(mesh):
    grid = Mesh(mesh.devices.reshape(NZ, NX, NY, NC), ALL)
    in_specs = (
        P(ALL, None),
        P(ALL, None),
        P(),
        P(),
        P(ALL),
        P(ROW, COL, None, None, None),
        P(ROW, COL, None),
        P(ROW, COL, None),
        P(ROW, COL),
    )
    out_specs = (P(ALL, None), P(ALL, None), P(), P())
    return jax.shard_map(body, mesh=grid, in_specs=in_specs, out_specs=out_specs, check_vma=False)
```

```python
import jax
import jax.numpy as jnp
from jax import lax
from jax.experimental import pallas as pl
from jax.experimental.pallas import tpu as pltpu
from jax.sharding import Mesh
from jax.sharding import PartitionSpec as P

NZ, NX, NY, NC = 8, 4, 8, 2
ALL = ("z", "x", "y", "core")
ROW = ("z", "x")
COL = ("y", "core")
B = 128
F = 128
WG = 32
BF = jnp.bfloat16
F32 = jnp.float32


def cost(us):
    return pl.CostEstimate(flops=0, bytes_accessed=int(us * 3.69e6), transcendentals=0)


VMEM = pl.BlockSpec(memory_space=pltpu.VMEM)
HBM = pl.BlockSpec(memory_space=pltpu.HBM)
ANY = pl.BlockSpec(memory_space=pl.ANY)
SMEM = pl.BlockSpec(memory_space=pltpu.SMEM)
PARAMS = pltpu.CompilerParams(vmem_limit_bytes=24 * 1024 * 1024)


def dot(a, b, contract=((1,), (0,))):
    return lax.dot_general(a, b, (contract, ((), ())), preferred_element_type=F32)


def forward_kernel(whole, bits, source, partial, acc, plan, sem):
    copy = pltpu.make_async_copy(whole, plan, sem)
    copy.start()
    acc[...] = jnp.zeros_like(acc)
    copy.wait()

    slots = bits.shape[0]
    products = [dot(bits[k], source[plan[0, k]]) for k in range(slots)]
    for k in range(slots):
        acc[plan[3, k]] += products[k]
    partial[...] = acc[: NX * NZ].astype(BF)


def forward_sums(plan, bits, source):
    return pl.pallas_call(
        forward_kernel,
        in_specs=[ANY, VMEM, VMEM],
        out_specs=VMEM,
        out_shape=jax.ShapeDtypeStruct((NX * NZ, B, F), BF),
        scratch_shapes=[
            pltpu.VMEM((NX * NZ + 1, B, F), F32),
            pltpu.SMEM(plan.shape, jnp.int32),
            pltpu.SemaphoreType.DMA,
        ],
        compiler_params=PARAMS,
        cost_estimate=cost(2.7),
        name="forward_sums",
    )(plan, bits, source)


def add_kernel(arrived, summed):
    total = arrived[0].astype(F32)
    for i in range(1, arrived.shape[0]):
        total += arrived[i].astype(F32)
    summed[...] = total.astype(BF)


def add_pieces(arrived):
    return pl.pallas_call(
        add_kernel,
        in_specs=[VMEM],
        out_specs=VMEM,
        out_shape=jax.ShapeDtypeStruct(arrived.shape[1:], BF),
        compiler_params=PARAMS,
        cost_estimate=cost(0.8),
        name="add_pieces",
    )(arrived)


def dense_kernel(
    pieces,
    features,
    cotangent,
    self_weight,
    neigh_weight,
    degrees,
    hidden,
    base,
    column,
    grads,
):
    total = pieces[0].astype(F32)
    for i in range(1, NZ):
        total += pieces[i].astype(F32)
    feats = features[...]
    inverse = lax.rsqrt(jnp.maximum(degrees[...], 1).astype(F32))
    mixed = (total * jnp.broadcast_to(inverse, (B, B)).T).astype(BF)
    linear = dot(feats, self_weight[...]) + dot(mixed, neigh_weight[...])
    sigma = jax.nn.sigmoid(linear)
    hidden[...] = (linear * sigma).astype(BF)
    grad = (cotangent[...].astype(F32) * sigma * (1.0 + linear * (1.0 - sigma))).astype(BF)
    spread = (dot(neigh_weight[...], grad, ((1,), (1,))) * inverse).astype(BF)
    base[...] = dot(self_weight[...], grad, ((1,), (1,)))
    column[...] = spread
    for i, left in enumerate((feats, mixed)):
        value = dot(left, grad, ((0,), (0,))).astype(BF)
        for j in range(NY // 2):
            grads[i * (NY // 2) + j] = value[j * WG : (j + 1) * WG]


def dense_layer(pieces, features, cotangent, self_weight, neigh_weight, degrees):
    return pl.pallas_call(
        dense_kernel,
        in_specs=[VMEM] * 6,
        out_specs=[VMEM] * 4,
        out_shape=[
            jax.ShapeDtypeStruct((B, F), BF),
            jax.ShapeDtypeStruct((F, B), F32),
            jax.ShapeDtypeStruct((F, B), BF),
            jax.ShapeDtypeStruct((NY, WG, F), BF),
        ],
        compiler_params=PARAMS,
        cost_estimate=cost(1.1),
        name="dense_layer",
    )(pieces, features, cotangent, self_weight, neigh_weight, degrees)


def pack_kernel(column, grads, payload):
    total = grads[0].astype(F32)
    for i in range(1, NY):
        total += grads[i].astype(F32)
    chunk = total.astype(BF)
    for i in range(NZ):
        payload[i, pl.ds(0, F)] = column[...]
        payload[i, pl.ds(F, WG)] = chunk


def pack(column, grads):
    return pl.pallas_call(
        pack_kernel,
        in_specs=[VMEM, VMEM],
        out_specs=VMEM,
        out_shape=jax.ShapeDtypeStruct((NZ, F + WG, B), BF),
        compiler_params=PARAMS,
        cost_estimate=cost(0.3),
        name="pack",
    )(column, grads)


def relay_kernel(arrived, payload):
    total = arrived[0, pl.ds(F, WG)].astype(F32)
    for i in range(1, NZ):
        total += arrived[i, pl.ds(F, WG)].astype(F32)
    chunk = total.astype(BF)
    for j in range(NX):
        for i in range(NZ):
            payload[j, pl.ds(i * F, F)] = arrived[i, pl.ds(0, F)]
        payload[j, pl.ds(NZ * F, WG)] = chunk


def relay(arrived):
    return pl.pallas_call(
        relay_kernel,
        in_specs=[VMEM],
        out_specs=VMEM,
        out_shape=jax.ShapeDtypeStruct((NX, NZ * F + WG, B), BF),
        compiler_params=PARAMS,
        cost_estimate=cost(1.0),
        name="relay",
    )(arrived)


def backward_kernel(whole, bits, spread, payload, acc, plan, sem):
    copy = pltpu.make_async_copy(whole, plan, sem)
    copy.start()
    acc[...] = jnp.zeros_like(acc)
    copy.wait()

    slots = bits.shape[0]
    products = []
    for k in range(slots):
        at = plan[1, k]
        block = spread[at // NZ, pl.ds(pl.multiple_of(at % NZ * F, F), F)]
        products.append(dot(block, bits[k]))
    for k in range(slots):
        acc[plan[2, k]] += products[k]
    tail = spread[0, pl.ds(NZ * F, WG)].astype(F32)
    for i in range(1, NX):
        tail += spread[i, pl.ds(NZ * F, WG)].astype(F32)
    for i in range(NY):
        for j in range(NC):
            payload[i, pl.ds(j * F, F)] = acc[j * NY + i].astype(BF)
        payload[i, pl.ds(NC * F, WG)] = tail.astype(BF)


def backward_sums(plan, bits, spread):
    return pl.pallas_call(
        backward_kernel,
        in_specs=[ANY, VMEM, VMEM],
        out_specs=VMEM,
        out_shape=jax.ShapeDtypeStruct((NY, NC * F + WG, B), BF),
        scratch_shapes=[
            pltpu.VMEM((NY * NC + 1, F, B), F32),
            pltpu.SMEM(plan.shape, jnp.int32),
            pltpu.SemaphoreType.DMA,
        ],
        compiler_params=PARAMS,
        cost_estimate=cost(1.5),
        name="backward_sums",
    )(plan, bits, spread)


def collect_kernel(arrived, sums):
    total = arrived[0, pl.ds(0, NC * F)].astype(F32)
    for i in range(1, NY):
        total += arrived[i, pl.ds(0, NC * F)].astype(F32)
    sums[pl.ds(0, NC * F)] = total.astype(BF)
    for i in range(NY):
        sums[pl.ds(NC * F + i * WG, WG)] = arrived[i, pl.ds(NC * F, WG)]


def collect(arrived):
    return pl.pallas_call(
        collect_kernel,
        in_specs=[VMEM],
        out_specs=VMEM,
        out_shape=jax.ShapeDtypeStruct((2 * NC * F, B), BF),
        compiler_params=PARAMS,
        cost_estimate=cost(0.3),
        name="collect",
    )(arrived)


def final_kernel(core, both, base, activated, hidden, grad_features, grad_self, grad_neigh):
    hidden[...] = activated[...]
    mine = pl.ds(pl.multiple_of(core[0] * F, F), F)
    total = base[...] + (both[0, mine].astype(F32) + both[1, mine].astype(F32))
    grad_features[...] = total.T.astype(BF)
    for i, out in ((NC, grad_self), (NC + 1, grad_neigh)):
        rows = pl.ds(i * F, F)
        out[...] = both[0, rows].astype(F32) + both[1, rows].astype(F32)


def final(core, both, base, activated):
    return pl.pallas_call(
        final_kernel,
        in_specs=[SMEM, VMEM, VMEM, VMEM],
        out_specs=[VMEM] * 4,
        out_shape=[
            jax.ShapeDtypeStruct((B, F), BF),
            jax.ShapeDtypeStruct((B, F), BF),
            jax.ShapeDtypeStruct((F, F), F32),
            jax.ShapeDtypeStruct((F, F), F32),
        ],
        compiler_params=PARAMS,
        cost_estimate=cost(0.8),
        name="final",
    )(core, both, base, activated)


def repeat_kernel(block, payload, held, sem, sems):
    load = pltpu.make_async_copy(block, held, sem)
    load.start()
    load.wait()
    copies = [pltpu.make_async_copy(held, payload.at[i], sems.at[i]) for i in range(NY)]
    for copy in copies:
        copy.start()
    for copy in copies:
        copy.wait()


def repeat(block):
    return pl.pallas_call(
        repeat_kernel,
        in_specs=[HBM],
        out_specs=HBM,
        out_shape=jax.ShapeDtypeStruct((NY, B, F), BF),
        scratch_shapes=[
            pltpu.VMEM((B, F), BF),
            pltpu.SemaphoreType.DMA,
            pltpu.SemaphoreType.DMA((NY,)),
        ],
        cost_estimate=cost(1.0),
        name="repeat",
    )(block)


def exchange(value, axis):
    return lax.all_to_all(value, axis, 0, 0, tiled=True)


def body(
    features,
    cotangent,
    self_weight,
    neigh_weight,
    degrees,
    adjacency,
    tile_rows,
    tile_cols,
    tile_count,
):
    slots = adjacency.shape[2]
    rows = tile_rows.reshape(slots)
    cols = tile_cols.reshape(slots)
    core = lax.axis_index("core")
    slot = jnp.arange(slots, dtype=jnp.int32)
    live = slot < tile_count.reshape(())
    col_at = cols % NC * NY + cols // NC
    row_at = rows % NX * NZ + rows // NX
    plan = jnp.stack(
        [
            col_at,
            row_at,
            jnp.where(live, col_at, NY * NC),
            jnp.where(live, row_at, NX * NZ),
            jnp.full_like(slot, core),
        ]
    )
    bits = adjacency.reshape(slots, B, B).astype(BF)

    near = exchange(repeat(features), "y")
    source = lax.all_gather(near, "core", axis=0, tiled=True)
    partial = forward_sums(plan, bits, source)
    arrived = exchange(partial.reshape(NX, NZ, B, F), "x")
    pieces = exchange(add_pieces(arrived), "z")
    activated, base, column, grads = dense_layer(
        pieces, features, cotangent, self_weight, neigh_weight, degrees.reshape(1, B)
    )
    payload = pack(column, exchange(grads, "y"))
    spread = exchange(relay(exchange(payload, "z")), "x")
    returned = exchange(backward_sums(plan, bits, spread), "y")
    both = lax.all_gather(collect(returned), "core", axis=0, tiled=False)
    return tuple(final(core.reshape(1), both, base, activated))


def solution(mesh):
    grid = Mesh(mesh.devices.reshape(NZ, NX, NY, NC), ALL)
    in_specs = (
        P(ALL, None),
        P(ALL, None),
        P(),
        P(),
        P(ALL),
        P(ROW, COL, None, None, None),
        P(ROW, COL, None),
        P(ROW, COL, None),
        P(ROW, COL),
    )
    out_specs = (P(ALL, None), P(ALL, None), P(), P())
    return jax.shard_map(body, mesh=grid, in_specs=in_specs, out_specs=out_specs, check_vma=False)
```

```python
import jax
import jax.numpy as jnp
from jax import lax
from jax.experimental import pallas as pl
from jax.experimental.pallas import tpu as pltpu
from jax.sharding import Mesh
from jax.sharding import PartitionSpec as P

NZ, NX, NY, NC = 8, 4, 8, 2
ALL = ("z", "x", "y", "core")
ROW = ("z", "x")
COL = ("y", "core")
B = 128
F = 128
WG = 32
BF = jnp.bfloat16
F32 = jnp.float32


def cost(us):
    return pl.CostEstimate(flops=0, bytes_accessed=int(us * 3.69e6), transcendentals=0)


VMEM = pl.BlockSpec(memory_space=pltpu.VMEM)
ANY = pl.BlockSpec(memory_space=pl.ANY)
SMEM = pl.BlockSpec(memory_space=pltpu.SMEM)
PARAMS = pltpu.CompilerParams(vmem_limit_bytes=24 * 1024 * 1024)


def dot(a, b, contract=((1,), (0,))):
    return lax.dot_general(a, b, (contract, ((), ())), preferred_element_type=F32)


def forward_kernel(whole, bits, source, partial, acc, plan, sem):
    copy = pltpu.make_async_copy(whole, plan, sem)
    copy.start()
    acc[...] = jnp.zeros_like(acc)
    copy.wait()

    slots = bits.shape[0]
    products = [dot(bits[k], source[plan[0, k]]) for k in range(slots)]
    for k in range(slots):
        acc[plan[3, k]] += products[k]
    partial[...] = acc[: NX * NZ].astype(BF)


def forward_sums(plan, bits, source):
    return pl.pallas_call(
        forward_kernel,
        in_specs=[ANY, VMEM, VMEM],
        out_specs=VMEM,
        out_shape=jax.ShapeDtypeStruct((NX * NZ, B, F), BF),
        scratch_shapes=[
            pltpu.VMEM((NX * NZ + 1, B, F), F32),
            pltpu.SMEM(plan.shape, jnp.int32),
            pltpu.SemaphoreType.DMA,
        ],
        compiler_params=PARAMS,
        cost_estimate=cost(2.7),
        name="forward_sums",
    )(plan, bits, source)


def add_kernel(arrived, summed):
    total = arrived[0].astype(F32)
    for i in range(1, arrived.shape[0]):
        total += arrived[i].astype(F32)
    summed[...] = total.astype(BF)


def add_pieces(arrived):
    return pl.pallas_call(
        add_kernel,
        in_specs=[VMEM],
        out_specs=VMEM,
        out_shape=jax.ShapeDtypeStruct(arrived.shape[1:], BF),
        compiler_params=PARAMS,
        cost_estimate=cost(0.8),
        name="add_pieces",
    )(arrived)


def dense_kernel(
    pieces,
    features,
    cotangent,
    self_weight,
    neigh_weight,
    degrees,
    hidden,
    base,
    column,
    grads,
):
    total = pieces[0].astype(F32)
    for i in range(1, NZ):
        total += pieces[i].astype(F32)
    feats = features[...]
    inverse = lax.rsqrt(jnp.maximum(degrees[...], 1).astype(F32))
    mixed = (total * jnp.broadcast_to(inverse, (B, B)).T).astype(BF)
    linear = dot(feats, self_weight[...]) + dot(mixed, neigh_weight[...])
    sigma = jax.nn.sigmoid(linear)
    hidden[...] = (linear * sigma).astype(BF)
    grad = (cotangent[...].astype(F32) * sigma * (1.0 + linear * (1.0 - sigma))).astype(BF)
    spread = (dot(neigh_weight[...], grad, ((1,), (1,))) * inverse).astype(BF)
    base[...] = dot(self_weight[...], grad, ((1,), (1,)))
    column[...] = spread
    for i, left in enumerate((feats, mixed)):
        value = dot(left, grad, ((0,), (0,))).astype(BF)
        for j in range(NY // 2):
            grads[i * (NY // 2) + j] = value[j * WG : (j + 1) * WG]


def dense_layer(pieces, features, cotangent, self_weight, neigh_weight, degrees):
    return pl.pallas_call(
        dense_kernel,
        in_specs=[VMEM] * 6,
        out_specs=[VMEM] * 4,
        out_shape=[
            jax.ShapeDtypeStruct((B, F), BF),
            jax.ShapeDtypeStruct((F, B), F32),
            jax.ShapeDtypeStruct((F, B), BF),
            jax.ShapeDtypeStruct((NY, WG, F), BF),
        ],
        compiler_params=PARAMS,
        cost_estimate=cost(1.1),
        name="dense_layer",
    )(pieces, features, cotangent, self_weight, neigh_weight, degrees)


def pack_kernel(column, grads, payload):
    total = grads[0].astype(F32)
    for i in range(1, NY):
        total += grads[i].astype(F32)
    chunk = total.astype(BF)
    for i in range(NZ):
        payload[i, pl.ds(0, F)] = column[...]
        payload[i, pl.ds(F, WG)] = chunk


def pack(column, grads):
    return pl.pallas_call(
        pack_kernel,
        in_specs=[VMEM, VMEM],
        out_specs=VMEM,
        out_shape=jax.ShapeDtypeStruct((NZ, F + WG, B), BF),
        compiler_params=PARAMS,
        cost_estimate=cost(0.3),
        name="pack",
    )(column, grads)


def relay_kernel(arrived, payload):
    total = arrived[0, pl.ds(F, WG)].astype(F32)
    for i in range(1, NZ):
        total += arrived[i, pl.ds(F, WG)].astype(F32)
    chunk = total.astype(BF)
    for j in range(NX):
        for i in range(NZ):
            payload[j, pl.ds(i * F, F)] = arrived[i, pl.ds(0, F)]
        payload[j, pl.ds(NZ * F, WG)] = chunk


def relay(arrived):
    return pl.pallas_call(
        relay_kernel,
        in_specs=[VMEM],
        out_specs=VMEM,
        out_shape=jax.ShapeDtypeStruct((NX, NZ * F + WG, B), BF),
        compiler_params=PARAMS,
        cost_estimate=cost(1.0),
        name="relay",
    )(arrived)


def backward_kernel(whole, bits, spread, payload, acc, plan, sem):
    copy = pltpu.make_async_copy(whole, plan, sem)
    copy.start()
    acc[...] = jnp.zeros_like(acc)
    copy.wait()

    slots = bits.shape[0]
    products = []
    for k in range(slots):
        at = plan[1, k]
        block = spread[at // NZ, pl.ds(pl.multiple_of(at % NZ * F, F), F)]
        products.append(dot(block, bits[k]))
    for k in range(slots):
        acc[plan[2, k]] += products[k]
    tail = spread[0, pl.ds(NZ * F, WG)].astype(F32)
    for i in range(1, NX):
        tail += spread[i, pl.ds(NZ * F, WG)].astype(F32)
    for i in range(NY):
        for j in range(NC):
            payload[i, pl.ds(j * F, F)] = acc[j * NY + i].astype(BF)
        payload[i, pl.ds(NC * F, WG)] = tail.astype(BF)


def backward_sums(plan, bits, spread):
    return pl.pallas_call(
        backward_kernel,
        in_specs=[ANY, VMEM, VMEM],
        out_specs=VMEM,
        out_shape=jax.ShapeDtypeStruct((NY, NC * F + WG, B), BF),
        scratch_shapes=[
            pltpu.VMEM((NY * NC + 1, F, B), F32),
            pltpu.SMEM(plan.shape, jnp.int32),
            pltpu.SemaphoreType.DMA,
        ],
        compiler_params=PARAMS,
        cost_estimate=cost(1.5),
        name="backward_sums",
    )(plan, bits, spread)


def collect_kernel(core, arrived, base, mine, packed):
    def target(k):
        rows = pl.ds(pl.multiple_of(k * F, F), F)
        total = arrived[0, rows].astype(F32)
        for i in range(1, NY):
            total += arrived[i, rows].astype(F32)
        return total

    mine[...] = base[...] + target(core[0])
    packed[pl.ds(0, F)] = target(1 - core[0]).astype(BF)
    for i in range(NY):
        packed[pl.ds(F + i * WG, WG)] = arrived[i, pl.ds(NC * F, WG)]


def collect(core, arrived, base):
    return pl.pallas_call(
        collect_kernel,
        in_specs=[SMEM, VMEM, VMEM],
        out_specs=[VMEM, VMEM],
        out_shape=[
            jax.ShapeDtypeStruct((F, B), F32),
            jax.ShapeDtypeStruct((F + NY * WG, B), BF),
        ],
        compiler_params=PARAMS,
        cost_estimate=cost(0.3),
        name="collect",
    )(core, arrived, base)


def final_kernel(core, both, base, activated, hidden, grad_features, grad_self, grad_neigh):
    hidden[...] = activated[...]
    total = base[...] + both[1 - core[0], pl.ds(0, F)].astype(F32)
    grad_features[...] = total.T.astype(BF)
    for i, out in ((1, grad_self), (2, grad_neigh)):
        rows = pl.ds(i * F, F)
        out[...] = both[0, rows].astype(F32) + both[1, rows].astype(F32)


def final(core, both, base, activated):
    return pl.pallas_call(
        final_kernel,
        in_specs=[SMEM, VMEM, VMEM, VMEM],
        out_specs=[VMEM] * 4,
        out_shape=[
            jax.ShapeDtypeStruct((B, F), BF),
            jax.ShapeDtypeStruct((B, F), BF),
            jax.ShapeDtypeStruct((F, F), F32),
            jax.ShapeDtypeStruct((F, F), F32),
        ],
        compiler_params=PARAMS,
        cost_estimate=cost(0.8),
        name="final",
    )(core, both, base, activated)


def exchange(value, axis):
    return lax.all_to_all(value, axis, 0, 0, tiled=True)


def body(
    features,
    cotangent,
    self_weight,
    neigh_weight,
    degrees,
    adjacency,
    tile_rows,
    tile_cols,
    tile_count,
):
    slots = adjacency.shape[2]
    rows = tile_rows.reshape(slots)
    cols = tile_cols.reshape(slots)
    core = lax.axis_index("core")
    slot = jnp.arange(slots, dtype=jnp.int32)
    live = slot < tile_count.reshape(())
    col_at = cols % NC * NY + cols // NC
    row_at = rows % NX * NZ + rows // NX
    plan = jnp.stack(
        [
            col_at,
            row_at,
            jnp.where(live, col_at, NY * NC),
            jnp.where(live, row_at, NX * NZ),
            jnp.full_like(slot, core),
        ]
    )
    bits = adjacency.reshape(slots, B, B).astype(BF)

    near = exchange(jnp.broadcast_to(features, (NY, B, F)), "y")
    source = lax.all_gather(near, "core", axis=0, tiled=True)
    partial = forward_sums(plan, bits, source)
    arrived = exchange(partial.reshape(NX, NZ, B, F), "x")
    pieces = exchange(add_pieces(arrived), "z")
    activated, base, column, grads = dense_layer(
        pieces, features, cotangent, self_weight, neigh_weight, degrees.reshape(1, B)
    )
    payload = pack(column, exchange(grads, "y"))
    spread = exchange(relay(exchange(payload, "z")), "x")
    returned = exchange(backward_sums(plan, bits, spread), "y")
    place = core.reshape(1)
    mine, packed = collect(place, returned, base)
    both = lax.all_gather(packed, "core", axis=0, tiled=False)
    return tuple(final(place, both, mine, activated))


def solution(mesh):
    grid = Mesh(mesh.devices.reshape(NZ, NX, NY, NC), ALL)
    in_specs = (
        P(ALL, None),
        P(ALL, None),
        P(),
        P(),
        P(ALL),
        P(ROW, COL, None, None, None),
        P(ROW, COL, None),
        P(ROW, COL, None),
        P(ROW, COL),
    )
    out_specs = (P(ALL, None), P(ALL, None), P(), P())
    return jax.shard_map(body, mesh=grid, in_specs=in_specs, out_specs=out_specs, check_vma=False)
```
